32 devices in a mesh: parts: 2 (over y), attn: 4 (over x, core), ffn: 4 (over z).
Axes of the slice: x: 2, y: 2, z: 4, core: 2. Of those that a mesh axis runs over, the one named last changes fastest.
Arguments:
- query: bfloat16 [4, 64, 16384], P(None, ('parts', 'attn'), 'ffn'), parts along dimension 1
- new_kv: bfloat16 [4, 64, 512], P(None, ('parts', 'attn')), parts along dimension 1
- kv_pool: bfloat16 [2048, 16, 512], P(('parts', 'attn')), parts along dimension 0, may hold values from -6 to 6
- kv_len: int32 [64], P(('parts', 'attn')), parts along dimension 0, may hold values from 1 to 512, as said below
- mig_dest: int32 [32], P('parts'), parts along dimension 0, may hold values from 0 to 3, as said below
- mig_from: int32 [32], P('parts'), parts along dimension 0, may hold values from 0 to 255
- mig_to: int32 [32], P('parts'), parts along dimension 0, may hold values from 0 to 255, as said below
- w_out: bfloat16 [16384, 7168], P('ffn', 'attn'), may hold values from -0.375 to 0.375
- norm_gain: bfloat16 [7168], P('attn'), may hold values from 0.099609375 to 1.8984375
- w_gate: bfloat16 [7168, 18432], P('attn', 'ffn'), may hold values from -0.0625 to 0.0625
- w_up: bfloat16 [7168, 18432], P('attn', 'ffn'), may hold values from -0.0625 to 0.0625
- w_down: bfloat16 [18432, 7168], P('ffn', 'attn'), may hold values from -0.046875 to 0.046875
- resid: bfloat16 [4, 64, 7168], P(None, 'parts', 'attn'), parts along dimension 1
Outputs:
- layer_out: bfloat16 [4, 64, 7168], P(None, ('parts', 'attn'), 'ffn'), parts along dimension 1
The draws below stay inside these ranges and needn't reach their ends.
There are 2 independent parts, one for each index of `parts`. The reference program is written for one: setup_inputs(seed, part) draws one part's arguments, and reference() takes and returns one part's arrays. A program takes and returns all parts, laid end to end along the dimension named above; an argument that names none is the same for every part. Nothing has to cross between parts.
Inputs may be any that keep to these rules, and one draw needn't show every extreme that they name: `kv_len`: some request holds exactly 512 positions in every draw. `mig_dest`: entry j belongs to attention device j // 4 and never names it; a device names 2 distinct destinations, each for exactly 2 of its entries. `mig_to`: no two entries with the same destination name the same destination block.
All inputs are finite; a program needn't handle non-finite values.
Results may differ from the reference program's by a relative error of at most 0.013.
Values may be sent and summed in bfloat16 or wider, within the bound.
A program may use at most 256 MiB of HBM per device.

```python
import math
import jax
import jax.numpy as jnp
from jax import lax

D = 7168
FF = 18432
HEADS = 64
HD = 256
R = 8
BS = 16
CAP = 2
STEPS = 4
ROWS = 32
NBLK = 256
CTX = 512
POOL = 1024
MIGS = 16
N_ATTN = 4
N_FFN = 4


def draw_query(key, part):
    key = jax.random.fold_in(key, 1)
    full_shape = (STEPS, ROWS, HEADS * HD)
    values_drawn = 1.5 * jax.random.normal(key, full_shape, jnp.float32)
    return values_drawn.astype(jnp.bfloat16)


def draw_new_kv(key, part):
    key = jax.random.fold_in(key, 2)
    full_shape = (STEPS, ROWS, 2 * HD)
    values_drawn = jax.random.normal(key, full_shape, jnp.float32)
    return values_drawn.astype(jnp.bfloat16)


def draw_resid(key, part):
    key = jax.random.fold_in(key, 3)
    position = jnp.arange(D, dtype=jnp.float32) / D
    column_scale = 0.2 * 10.0 ** position * jnp.exp(jax.random.uniform(jax.random.fold_in(key, 1), (D,), jnp.float32, 0.0, math.log(3.0)))
    row_scale = 0.2 * jnp.exp(jax.random.uniform(jax.random.fold_in(key, 2), (ROWS,), jnp.float32, 0.0, math.log(10.0)))
    noise_draw = jax.random.normal(jax.random.fold_in(key, 3), (STEPS, ROWS, D), jnp.float32)
    return (noise_draw * row_scale[None, :, None] * column_scale[None, None, :]).astype(jnp.bfloat16)


def draw_kv_len(key, part):
    key = jax.random.fold_in(key, 4)
    device_cap = jax.random.randint(jax.random.fold_in(key, 1), (N_ATTN,), CTX // 4, CTX + 1)
    raw_draw = jax.random.randint(jax.random.fold_in(key, 2), (ROWS,), 0, 1 << 20)
    lengths = 1 + raw_draw % jnp.repeat(device_cap, R, total_repeat_length=ROWS)
    longest = jax.random.randint(jax.random.fold_in(key, 3), (), 0, ROWS)
    return jnp.where(jnp.arange(ROWS) == longest, CTX, lengths).astype(jnp.int32)


def shuffle_peers(sub_key):
    return jax.random.permutation(sub_key, N_ATTN - 1)


def shuffle_blocks(sub_key):
    return jax.random.permutation(sub_key, NBLK)


def migration_plan(key):
    per_source = CAP * (N_ATTN // 2)
    peer_keys = jax.random.split(jax.random.fold_in(key, 201), N_ATTN)
    offsets = jax.vmap(shuffle_peers)(peer_keys)
    group_index = jnp.arange(per_source) // CAP
    destination = (jnp.arange(N_ATTN)[:, None] + 1 + offsets[:, group_index]) % N_ATTN
    destination = destination.reshape(-1).astype(jnp.int32)
    block_keys = jax.random.split(jax.random.fold_in(key, 202), N_ATTN)
    orders = jax.vmap(shuffle_blocks)(block_keys)
    onehot = (destination[:, None] == jnp.arange(N_ATTN)[None, :]).astype(jnp.int32)
    before = jnp.cumsum(onehot, axis=0) - onehot
    arrival = jnp.sum(before * onehot, axis=1)
    block_slots = orders[destination, arrival]
    return (destination, block_slots.astype(jnp.int32))


def draw_mig_dest(key, part):
    destination, block_slots = migration_plan(key)
    return destination


def draw_mig_to(key, part):
    destination, block_slots = migration_plan(key)
    return block_slots


def with_ends(result, stream_key, low, top_value):
    longest = result.shape.index(max(result.shape))
    spots = []
    for shift in (0, 1):
        where = [jax.random.randint(jax.random.fold_in(stream_key, axis), (), 0, length) for axis, length in enumerate(result.shape)]
        where[longest] = (where[longest] + shift) % result.shape[longest]
        spots.append(tuple(where))
    return result.at[spots[0]].set(low).at[spots[1]].set(top_value)


def block_levels(key, dims, cuts, least, top_value):
    def one(dim, blocks):
        heights = jax.random.uniform(jax.random.fold_in(jax.random.fold_in(key, 6), dim), (blocks,), jnp.float32, least / len(cuts), top_value / len(cuts))
        return jnp.repeat(jnp.exp(heights), dims[dim] // blocks).reshape((-1,) + (1,) * (len(dims) - dim - 1))

    level = one(*cuts[0])
    for cut in cuts[1:]:
        level = level * one(*cut)
    return level


def gaussian(key, dims, deviation, most, cuts=(), kind=jnp.bfloat16):
    array = jax.random.normal(key, dims, jnp.float32) * deviation
    if len(cuts) > 0:
        array = block_levels(key, dims, cuts, -0.22, 0.18) * array
    return jnp.clip(array, min=-most, max=most).astype(kind)


def setup_inputs(seed: int = 0, part: int = 0) -> dict:
    key_list = jax.random.split(jax.random.key(seed), 14)
    part_keys = jax.random.split(jax.random.fold_in(key_list[13], part), 14)
    return {
        "query": draw_query(jax.random.fold_in(jax.random.fold_in(key_list[13], part), 71), part),
        "new_kv": draw_new_kv(jax.random.fold_in(jax.random.fold_in(key_list[13], part), 71), part),
        "kv_pool": gaussian(part_keys[2], (POOL, BS, 2 * HD), 1.0, 6.0, ((0, 4),)),
        "kv_len": draw_kv_len(jax.random.fold_in(jax.random.fold_in(key_list[13], part), 71), part),
        "mig_dest": draw_mig_dest(jax.random.fold_in(jax.random.fold_in(key_list[13], part), 71), part),
        "mig_from": with_ends(jax.random.randint(part_keys[5], (MIGS,), 0, NBLK), jax.random.fold_in(part_keys[5], 1), 0, NBLK - 1).astype(jnp.int32),
        "mig_to": draw_mig_to(jax.random.fold_in(jax.random.fold_in(key_list[13], part), 71), part),
        "w_out": gaussian(key_list[7], (HEADS * HD, D), (HEADS * HD // 64) ** -0.5, 0.375, ((0, 4), (1, 4))),
        "norm_gain": jnp.clip(1.0 + 0.18 * jax.random.normal(key_list[8], (D,), jnp.float32), 0.099609375, 1.8984375).astype(jnp.bfloat16),
        "w_gate": gaussian(key_list[9], (D, FF), D ** -0.5, 0.0625, ((0, 4), (1, 4))),
        "w_up": gaussian(key_list[10], (D, FF), D ** -0.5, 0.0625, ((0, 4), (1, 4))),
        "w_down": gaussian(key_list[11], (FF, D), FF ** -0.5, 0.046875, ((0, 4), (1, 4))),
        "resid": draw_resid(jax.random.fold_in(jax.random.fold_in(key_list[13], part), 71), part),
    }


def stored(value):
    return lax.optimization_barrier(value.astype(jnp.bfloat16)).astype(jnp.float32)

def attend(queries, cache_kv, lengths, fresh_kv, head_dim):
    row_count = queries.shape[0]
    per_head = queries.reshape(row_count, -1, head_dim).astype(jnp.float32)
    key_part = cache_kv[:, :, :head_dim].astype(jnp.float32)
    value_part = cache_kv[:, :, head_dim:].astype(jnp.float32)
    score_scale = head_dim ** (-0.5)
    cache_scores = jnp.einsum('rhd,rcd->rhc', per_head, key_part) * score_scale
    position = jnp.arange(cache_kv.shape[1], dtype=jnp.int32)
    live_mask = position[None, None, :] < lengths[:, None, None]
    cache_scores = jnp.where(live_mask, cache_scores, -jnp.inf)
    fresh_keys = fresh_kv[:, :, :head_dim].astype(jnp.float32)
    fresh_values = fresh_kv[:, :, head_dim:].astype(jnp.float32)
    recent_scores = jnp.einsum('rhd,srd->rhs', per_head, fresh_keys) * score_scale
    row_max = jnp.maximum(lax.optimization_barrier(jnp.max(cache_scores, axis=2)), lax.optimization_barrier(jnp.max(recent_scores, axis=2)))
    cache_probs = jnp.exp(cache_scores - row_max[:, :, None])
    recent_probs = jnp.exp(recent_scores - row_max[:, :, None])
    weight_sum = lax.optimization_barrier(jnp.sum(cache_probs, axis=2)) + lax.optimization_barrier(jnp.sum(recent_probs, axis=2))
    weighted = jnp.einsum('rhc,rcd->rhd', stored(cache_probs), value_part)
    weighted = weighted + jnp.einsum('rhs,srd->rhd', stored(recent_probs), fresh_values)
    return (weighted / weight_sum[:, :, None]).astype(jnp.bfloat16).reshape(row_count, -1)

def grouped(left_side, right_side, groups):
    group_width = left_side.shape[1] // groups
    summed = jnp.zeros((left_side.shape[0], right_side.shape[1]), jnp.float32)
    for group in range(groups):
        lo_edge = group * group_width
        product = jnp.dot(left_side[:, lo_edge:lo_edge + group_width], right_side[lo_edge:lo_edge + group_width], preferred_element_type=jnp.float32)
        summed = summed + stored(product)
    return summed

def reference(query, new_kv, kv_pool, kv_len, mig_dest, mig_from, mig_to, w_out, norm_gain, w_gate, w_up, w_down, resid):
    blocks = kv_pool.shape[0] // N_ATTN
    per_source = mig_dest.shape[0] // N_ATTN
    source = jnp.arange(mig_dest.shape[0], dtype=jnp.int32) // per_source
    anchor = source * blocks + mig_from
    target = mig_dest * blocks + mig_to
    moved_pool = kv_pool.at[target].set(kv_pool[anchor])
    row_count = kv_len.shape[0]
    cache_kv = moved_pool.reshape(row_count, -1, kv_pool.shape[2])
    head_dim = kv_pool.shape[2] // 2
    outputs = []
    for decode_step in range(STEPS):
        attended = attend(query[decode_step], cache_kv, kv_len, new_kv[:decode_step + 1], head_dim)
        head_sum = grouped(attended, w_out, N_FFN)
        state_bf = (resid[decode_step].astype(jnp.float32) + head_sum).astype(jnp.bfloat16)
        widened = state_bf.astype(jnp.float32)
        squares = lax.optimization_barrier(jnp.sum(widened * widened, axis=1, keepdims=True))
        normed = (widened * lax.rsqrt(squares / widened.shape[1] + 1e-06) * norm_gain.astype(jnp.float32)).astype(jnp.bfloat16)
        gate_sum = grouped(normed, w_gate, N_ATTN)
        up_sum = grouped(normed, w_up, N_ATTN)
        hidden = (jax.nn.silu(gate_sum) * up_sum).astype(jnp.bfloat16)
        ffn_sum = grouped(hidden, w_down, N_FFN)
        outputs.append((widened + ffn_sum).astype(jnp.bfloat16))
    return jnp.stack(outputs)
```

```python
import jax
import jax.numpy as jnp
from jax import lax
from jax.experimental import pallas as pl
from jax.experimental.pallas import tpu as pltpu
from jax.sharding import PartitionSpec as P

D = 7168
CAP = 2
STEPS = 4


def stored(value):
    return lax.optimization_barrier(value.astype(jnp.bfloat16)).astype(jnp.float32)


def attend_local(queries, cache_kv, lengths, fresh_kv, head_dim):
    row_count = queries.shape[0]
    per_head = queries.reshape(row_count, -1, head_dim)
    key_part = cache_kv[:, :, :head_dim]
    value_part = cache_kv[:, :, head_dim:]
    score_scale = head_dim ** (-0.5)
    cache_scores = (
        jnp.einsum("rhd,rcd->rhc", per_head, key_part, preferred_element_type=jnp.float32)
        * score_scale
    )
    position = jnp.arange(cache_kv.shape[1], dtype=jnp.int32)
    live_mask = position[None, None, :] < lengths[:, None, None]
    cache_scores = jnp.where(live_mask, cache_scores, -jnp.inf)
    fresh_keys = fresh_kv[:, :, :head_dim]
    fresh_values = fresh_kv[:, :, head_dim:]
    recent_scores = (
        jnp.einsum("rhd,srd->rhs", per_head, fresh_keys, preferred_element_type=jnp.float32)
        * score_scale
    )
    row_max = jnp.maximum(jnp.max(cache_scores, axis=2), jnp.max(recent_scores, axis=2))
    cache_probs = jnp.exp(cache_scores - row_max[:, :, None])
    recent_probs = jnp.exp(recent_scores - row_max[:, :, None])
    weight_sum = jnp.sum(cache_probs, axis=2) + jnp.sum(recent_probs, axis=2)
    weighted = jnp.einsum(
        "rhc,rcd->rhd",
        cache_probs.astype(jnp.bfloat16),
        value_part,
        preferred_element_type=jnp.float32,
    )
    weighted = weighted + jnp.einsum(
        "rhs,srd->rhd",
        recent_probs.astype(jnp.bfloat16),
        fresh_values,
        preferred_element_type=jnp.float32,
    )
    return (weighted / weight_sum[:, :, None]).astype(jnp.bfloat16).reshape(row_count, -1)


def body(
    query,
    new_kv,
    kv_pool,
    kv_len,
    mig_dest,
    mig_from,
    mig_to,
    w_out,
    norm_gain,
    w_gate,
    w_up,
    w_down,
    resid,
):
    peer_count = lax.axis_size("attn")
    my_index = lax.axis_index("attn")
    blocks = kv_pool.shape[0]
    feature_width = kv_pool.shape[2]
    entries = mig_dest.shape[0]
    per_source = entries // peer_count
    entry_index = jnp.arange(entries, dtype=jnp.int32)
    source = entry_index // per_source
    pair_key = source * peer_count + mig_dest
    earlier = (pair_key[:, None] == pair_key[None, :]) & (
        entry_index[None, :] < entry_index[:, None]
    )
    pair_rank = jnp.sum(earlier.astype(jnp.int32), axis=1)
    my_dest = lax.dynamic_slice_in_dim(mig_dest, my_index * per_source, per_source)
    my_from = lax.dynamic_slice_in_dim(mig_from, my_index * per_source, per_source)
    my_rank = lax.dynamic_slice_in_dim(pair_rank, my_index * per_source, per_source)
    send_slot = my_dest * CAP + my_rank
    outgoing = jnp.zeros((peer_count * CAP, kv_pool.shape[1], feature_width), jnp.bfloat16)
    outgoing = (
        outgoing.at[send_slot]
        .set(kv_pool[my_from])
        .reshape(peer_count, CAP, kv_pool.shape[1], feature_width)
    )
    land_slot = jnp.where(mig_dest == my_index, source * CAP + pair_rank, peer_count * CAP)
    landing = (
        jnp.full((peer_count * CAP,), blocks, jnp.int32).at[land_slot].set(mig_to, mode="drop")
    )
    arrived = lax.all_to_all(outgoing, "attn", split_axis=0, concat_axis=0, tiled=True)
    received = arrived.reshape(peer_count * CAP, kv_pool.shape[1], feature_width)
    new_pool = kv_pool.at[landing].set(received, mode="drop")
    cache_kv = new_pool.reshape(kv_len.shape[0], -1, feature_width)
    head_dim = feature_width // 2
    paired = jnp.concatenate([w_gate, w_up], axis=1)
    unit_count = w_gate.shape[1]
    lane_count = lax.axis_size("ffn")
    lane_index = lax.axis_index("ffn")
    outputs = []
    for decode_step in range(STEPS):
        attended = attend_local(
            query[decode_step], cache_kv, kv_len, new_kv[: decode_step + 1], head_dim
        )
        head_part = jnp.dot(
            lax.all_gather(attended, "attn", axis=0, tiled=True),
            w_out,
            preferred_element_type=jnp.float32,
        ).astype(jnp.bfloat16)
        head_sum = lax.psum(head_part.astype(jnp.float32).astype(jnp.bfloat16), "ffn").astype(
            jnp.float32
        )
        state_bf = (resid[decode_step].astype(jnp.float32) + head_sum).astype(jnp.bfloat16)
        widened = state_bf.astype(jnp.float32)
        squares = lax.psum(jnp.sum(widened * widened, axis=1), "attn")
        normed = (
            widened * lax.rsqrt(squares[:, None] / D + 1e-06) * norm_gain.astype(jnp.float32)
        ).astype(jnp.bfloat16)
        gate_up = lax.psum_scatter(
            stored(jnp.dot(normed, paired, preferred_element_type=jnp.float32)).astype(
                jnp.bfloat16
            ),
            "attn",
            scatter_dimension=0,
            tiled=True,
        ).astype(jnp.float32)
        hidden = (jax.nn.silu(gate_up[:, :unit_count]) * gate_up[:, unit_count:]).astype(
            jnp.bfloat16
        )
        unit_part = jnp.dot(
            lax.all_gather(hidden, "attn", axis=0, tiled=True),
            w_down,
            preferred_element_type=jnp.float32,
        ).astype(jnp.bfloat16)
        unit_sum = lax.psum(unit_part.astype(jnp.float32).astype(jnp.bfloat16), "ffn").astype(
            jnp.float32
        )
        layer_out = (widened + unit_sum).astype(jnp.bfloat16)
        by_row = lax.all_to_all(layer_out, "attn", split_axis=0, concat_axis=1, tiled=True)
        share_width = by_row.shape[1] // lane_count
        outputs.append(lax.dynamic_slice_in_dim(by_row, lane_index * share_width, share_width, 1))
    return jnp.stack(outputs)


MESH = pl.DeviceIdType.MESH
CHUNKS = 6
SLOTS = 4
COLS = 256


def near_of(i):
    return i + 1 - 2 * lax.rem(i, 2)


def far_of(i):
    return lax.rem(i + 2, 4)


def layer_kernel(
    table,
    sends,
    lengths,
    query,
    new_kv,
    resid,
    gain,
    pool_hbm,
    w_out,
    w_gate,
    w_up,
    w_down,
    out,
    pool,
    stage,
    land,
    cache,
    q_rows,
    fresh,
    att_rows,
    att,
    wide,
    part,
    zsend,
    zrecv,
    state,
    lhs,
    sq_send,
    sq_recv,
    wbig,
    wgu,
    gu_keep,
    gu_send,
    gu_recv,
    gx_send,
    gx_recv,
    hid,
    acc,
    tsend,
    lsem,
    ssem,
    rsem,
):
    a = lax.axis_index("attn")
    f = lax.axis_index("ffn")
    p = lax.axis_index("parts")
    an, af = near_of(a), far_of(a)
    fn, ff = near_of(f), far_of(f)
    aff, fff = far_of(an), far_of(fn)
    blocks = pool_hbm.shape[0]
    reqs = lengths.shape[0]
    steps = query.shape[0]
    rows = steps * reqs
    hd = pool_hbm.shape[2] // 2
    heads = query.shape[2] // hd
    qlen = steps * heads
    width = w_out.shape[1]
    units = w_gate.shape[1]
    cu = units // CHUNKS
    per_req = blocks // reqs
    bs = pool_hbm.shape[1]

    def at_attn(i):
        return (p, i, f)

    def at_ffn(i):
        return (p, a, i)

    def remote(k, src, dst, dev):
        return pltpu.make_async_remote_copy(
            src_ref=src,
            dst_ref=dst,
            send_sem=ssem.at[k],
            recv_sem=rsem.at[k],
            device_id=dev,
            device_id_type=MESH,
        )

    def gu_load(c):
        s = c % SLOTS
        return [
            pltpu.make_async_copy(
                w.at[:, pl.ds(c * cu, cu)], wgu.at[s, j], lsem.at[2 + s * 2 + j]
            )
            for j, w in enumerate((w_gate, w_up))
        ]

    pool_load = pltpu.make_async_copy(pool_hbm, pool.at[pl.ds(0, blocks)], lsem.at[0])
    pool_load.start()
    out_load = pltpu.make_async_copy(w_out, wbig.at[pl.ds(0, w_out.shape[0])], lsem.at[1])
    out_load.start()
    for c in range(SLOTS):
        for d in gu_load(c):
            d.start()

    barrier = pltpu.get_barrier_semaphore()
    moved = a != f
    for o in range(1, 4):
        pl.semaphore_signal(
            barrier, inc=1, device_id=at_attn(lax.rem(a + o, 4)), device_id_type=MESH
        )
    for peer in (fn, ff):
        pl.semaphore_signal(barrier, inc=1, device_id=at_ffn(peer), device_id_type=MESH)

    @pl.when(moved)
    def _():
        pl.semaphore_signal(barrier, inc=1, device_id=(p, f, a), device_id_type=MESH)
        pl.semaphore_wait(barrier, 6)

    @pl.when(jnp.logical_not(moved))
    def _():
        pl.semaphore_wait(barrier, 5)

    pool_load.wait()
    mig = []
    for o in range(1, 4):
        d = lax.rem(a + o, 4)
        for s in range(CAP):
            stage[o - 1, s] = pool[sends[d * CAP + s]]
        mig.append(
            remote(o - 1, stage.at[o - 1], land.at[pl.ds(CAP * a, CAP)], at_attn(d))
        )
        mig[-1].start()

    for t in range(steps):
        q_t = query[t].astype(jnp.float32)
        for h in range(heads):
            for half in range(2):
                lo = h * hd + half * 128
                q_rows[half, pl.ds(t * heads + h, reqs, stride=qlen), :] = q_t[:, lo : lo + 128]
    fresh[...] = jnp.zeros_like(fresh)
    for t in range(steps):
        fresh_t = new_kv[t].astype(jnp.float32)
        for half in range(4):
            fresh[half, pl.ds(t, reqs, stride=16), :] = fresh_t[:, half * 128 : (half + 1) * 128]
    for t in range(steps):
        wide[t] = resid[t].astype(jnp.float32)

    land[pl.ds(CAP * a, CAP)] = jnp.zeros((CAP, bs, 2 * hd), jnp.bfloat16)
    for copy in mig:
        copy.wait()
    pool[pl.ds(blocks, 4 * CAP)] = land[...]

    scale = hd ** (-0.5)

    def one_request(i, carry):
        for b in range(per_req):
            cache[b * bs : (b + 1) * bs, :] = pool[table[i * per_req + b]]
        mine = pl.ds(i * qlen, qlen)
        q = jnp.concatenate([q_rows[0, mine, :], q_rows[1, mine, :]], axis=1).astype(jnp.bfloat16)
        contract = (((1,), (1,)), ((), ()))
        s1 = (
            lax.dot_general(q, cache[:, :hd], contract, preferred_element_type=jnp.float32)
            * scale
        )
        pos = lax.broadcasted_iota(jnp.int32, s1.shape, 1)
        s1 = jnp.where(pos < lengths[i], s1, -jnp.inf)
        at = pl.ds(i * 16, 16)
        fk = jnp.concatenate([fresh[0, at, :], fresh[1, at, :]], axis=1).astype(jnp.bfloat16)
        fv = jnp.concatenate([fresh[2, at, :], fresh[3, at, :]], axis=1).astype(jnp.bfloat16)
        s2 = lax.dot_general(q, fk, contract, preferred_element_type=jnp.float32) * scale
        step_of = lax.broadcasted_iota(jnp.int32, s2.shape, 0) // heads
        s2 = jnp.where(lax.broadcasted_iota(jnp.int32, s2.shape, 1) <= step_of, s2, -jnp.inf)
        top = jnp.maximum(
            jnp.max(s1, axis=1, keepdims=True), jnp.max(s2, axis=1, keepdims=True)
        )
        p1 = jnp.exp(s1 - top)
        p2 = jnp.exp(s2 - top)
        total = jnp.sum(p1, axis=1, keepdims=True) + jnp.sum(p2, axis=1, keepdims=True)
        o = jnp.dot(
            p1.astype(jnp.bfloat16), cache[:, hd:], preferred_element_type=jnp.float32
        ) + jnp.dot(p2.astype(jnp.bfloat16), fv, preferred_element_type=jnp.float32)
        o = o / total
        for half in range(2):
            att_rows[half, pl.ds(i * qlen, qlen), :] = o[:, half * 128 : (half + 1) * 128]
        return carry

    lax.fori_loop(0, reqs, one_request, 0)

    for h in range(heads):
        for half in range(2):
            lo = h * hd + half * 128
            att[a, :, lo : lo + 128] = jnp.concatenate(
                [
                    att_rows[half, pl.ds(t * heads + h, reqs, stride=qlen), :]
                    for t in range(steps)
                ],
                axis=0,
            ).astype(jnp.bfloat16)

    def gather_begin(k, at, me, near, far, dev):
        own = [remote(k + 1, at(me), at(me), dev(far)), remote(k, at(me), at(me), dev(near))]
        for copy in own:
            copy.start()
        return own

    def gather_relay(k, own, at, near, far, dev):
        own[0].wait_recv()
        relay = remote(k + 2, at(far), at(far), dev(near))
        relay.start()
        return own + [relay]

    def gather_end(copies):
        copies[1].wait_recv()
        copies[2].wait_recv()
        for copy in copies:
            copy.wait_send()

    own = gather_begin(3, lambda i: att.at[i], a, an, af, at_attn)
    own = gather_relay(3, own, lambda i: att.at[i], an, af, at_attn)
    out_load.wait()
    gather_end(own)

    tiles = width // COLS
    half_tiles = ((tiles + 1) // 2, tiles // 2)
    col_cuts = ((0, half_tiles[0] * COLS), (half_tiles[0] * COLS, width))

    def out_tile(j, carry):
        at = pl.ds(pl.multiple_of(j * COLS, COLS), COLS)
        r = jnp.dot(
            att[...].reshape(4 * rows, att.shape[2]),
            wbig[: w_out.shape[0], at],
            preferred_element_type=jnp.float32,
        )
        part[:, :, at] = r.reshape(4, rows, COLS)
        return carry

    def reduce_near(k, z, lo, hi):
        zsend[z, 0, :, lo:hi] = part[fff, :, lo:hi].astype(jnp.bfloat16)
        zsend[z, 1, :, lo:hi] = part[fn, :, lo:hi].astype(jnp.bfloat16)
        copies = []
        for j in range(2):
            piece = (z, j, slice(None), pl.ds(lo, hi - lo))
            copies.append(remote(k + j, zsend.at[piece], zrecv.at[piece], at_ffn(fn)))
            copies[-1].start()
        return copies

    def reduce_far(k, z, lo, hi, copies):
        copies[0].wait_recv()
        zsend[z, 2, :, lo:hi] = (
            part[ff, :, lo:hi] + zrecv[z, 0, :, lo:hi].astype(jnp.float32)
        ).astype(jnp.bfloat16)
        piece = (z, 2, slice(None), pl.ds(lo, hi - lo))
        copy = remote(k + 2, zsend.at[piece], zrecv.at[piece], at_ffn(ff))
        copy.start()
        return copies + [copy]

    def reduce_end(z, lo, hi, copies):
        copies[1].wait_recv()
        copies[2].wait_recv()
        total = (
            part[f, :, lo:hi]
            + zrecv[z, 1, :, lo:hi].astype(jnp.float32)
            + zrecv[z, 2, :, lo:hi].astype(jnp.float32)
        )
        for copy in copies:
            copy.wait_send()
        return total

    def state_at(lo, hi):
        return lambda i: state.at[i, :, pl.ds(lo, hi - lo)]

    def make_state(lo, hi, total):
        base = jnp.concatenate(
            [wide[t, pl.ds(pl.multiple_of(f * reqs, reqs), reqs), lo:hi] for t in range(steps)],
            axis=0,
        )
        state[f, :, lo:hi] = (base + total).astype(jnp.bfloat16)

    (l0, h0), (l1, h1) = col_cuts
    lax.fori_loop(0, half_tiles[0], out_tile, 0)
    r0 = reduce_near(6, 0, l0, h0)
    lax.fori_loop(half_tiles[0], tiles, out_tile, 0)
    down_load = pltpu.make_async_copy(w_down, wbig, lsem.at[1])
    down_load.start()
    r1 = reduce_near(9, 0, l1, h1)
    r0 = reduce_far(6, 0, l0, h0, r0)
    r1 = reduce_far(9, 0, l1, h1, r1)
    make_state(l0, h0, reduce_end(0, l0, h0, r0))
    g0 = gather_begin(12, state_at(l0, h0), f, fn, ff, at_ffn)
    make_state(l1, h1, reduce_end(0, l1, h1, r1))
    g1 = gather_begin(15, state_at(l1, h1), f, fn, ff, at_ffn)
    g0 = gather_relay(12, g0, state_at(l0, h0), fn, ff, at_ffn)
    g1 = gather_relay(15, g1, state_at(l1, h1), fn, ff, at_ffn)
    gather_end(g0)
    gather_end(g1)

    gain_f = gain[...].astype(jnp.float32)

    def scale_rows(i, carry):
        w = state[i].astype(jnp.float32)
        lhs[i] = (w * gain_f).astype(jnp.bfloat16)
        sq_send[i] = jnp.broadcast_to(jnp.sum(w * w, axis=1, keepdims=True), (rows, 128))
        return carry

    lax.fori_loop(0, 4, scale_rows, 0)
    sq = []
    for o in range(1, 4):
        d = lax.rem(a + o, 4)
        sq.append(remote(17 + o, sq_send.at[d], sq_recv.at[a], at_attn(d)))
        sq[-1].start()
    sq_recv[a] = sq_send[a]

    K = 21
    near_copy, far_copy, hid_copy = {}, {}, {}

    def hid_at(c):
        return lambda i: hid.at[c, i]

    def stage_matmul(c):
        s = c % SLOTS
        for d in gu_load(c):
            d.wait()

        for j in range(2):

            def tile(n, carry):
                at = pl.ds(pl.multiple_of(n * COLS, COLS), COLS)
                to = pl.ds(pl.multiple_of(j * cu + n * COLS, COLS), COLS)
                gu_keep[c % 2, :, :, to] = jnp.dot(
                    lhs[...].reshape(4 * rows, width),
                    wgu[s, j, :, at],
                    preferred_element_type=jnp.float32,
                ).reshape(4, rows, COLS)
                return carry

            lax.fori_loop(0, cu // COLS, tile, 0)
        if c + SLOTS < CHUNKS:
            for d in gu_load(c + SLOTS):
                d.start()
        gu_send[c, 0] = gu_keep[c % 2, aff].astype(jnp.bfloat16)
        gu_send[c, 1] = gu_keep[c % 2, an].astype(jnp.bfloat16)
        near_copy[c] = remote(K + c, gu_send.at[c], gu_recv.at[c], at_attn(an))
        near_copy[c].start()

    def stage_far(c):
        near_copy[c].wait()
        gx_send[c] = (gu_keep[c % 2, af] + gu_recv[c, 0].astype(jnp.float32)).astype(
            jnp.bfloat16
        )
        far_copy[c] = remote(K + CHUNKS + c, gx_send.at[c], gx_recv.at[c], at_attn(af))
        far_copy[c].start()
        gu_keep[c % 2, a] = gu_keep[c % 2, a] + gu_recv[c, 1].astype(jnp.float32)

    def stage_hidden(c, rs):
        far_copy[c].wait()
        gu = gu_keep[c % 2, a] + gx_recv[c].astype(jnp.float32)
        g = gu[:, :cu] * rs
        u = gu[:, cu:] * rs
        hid[c, a] = (g / (1.0 + jnp.exp(-g)) * u).astype(jnp.bfloat16)
        hid_copy[c] = gather_begin(K + 2 * CHUNKS + 3 * c, hid_at(c), a, an, af, at_attn)

    def stage_relay(c):
        hid_copy[c] = gather_relay(
            K + 2 * CHUNKS + 3 * c, hid_copy[c], hid_at(c), an, af, at_attn
        )

    def stage_down(c):
        gather_end(hid_copy[c])

        def tile(n, carry):
            at = pl.ds(pl.multiple_of(n * COLS, COLS), COLS)
            r = jnp.dot(
                hid[c].reshape(4 * rows, cu),
                wbig[c * cu : (c + 1) * cu, at],
                preferred_element_type=jnp.float32,
            ).reshape(4, rows, COLS)
            if c == 0:
                part[:, :, at] = r
            else:
                part[:, :, at] = part[:, :, at] + r
            return carry

        lax.fori_loop(0, width // COLS, tile, 0)

    stage_matmul(0)
    stage_far(0)
    for copy in sq:
        copy.wait()
    squares = sq_recv[0] + sq_recv[1] + sq_recv[2] + sq_recv[3]
    rs = lax.rsqrt(squares[:, :1] / D + 1e-06)
    stage_matmul(1)
    stage_far(1)
    stage_hidden(0, rs)
    for c in range(2, CHUNKS):
        stage_matmul(c)
        stage_far(c)
        stage_hidden(c - 1, rs)
        stage_relay(c - 2)
        if c == 3:
            down_load.wait()
        if c >= 3:
            stage_down(c - 3)
    stage_relay(CHUNKS - 2)
    stage_down(CHUNKS - 3)
    stage_hidden(CHUNKS - 1, rs)
    stage_down(CHUNKS - 2)
    stage_relay(CHUNKS - 1)
    stage_down(CHUNKS - 1)

    K2 = K + 5 * CHUNKS
    d0 = reduce_near(K2, 1, l0, h0)
    d1 = reduce_near(K2 + 3, 1, l1, h1)
    d0 = reduce_far(K2, 1, l0, h0, d0)
    d1 = reduce_far(K2 + 3, 1, l1, h1, d1)
    for lo, hi, d in ((l0, h0, d0), (l1, h1, d1)):
        total = reduce_end(1, lo, hi, d)
        tsend[:, lo:hi] = (state[f, :, lo:hi].astype(jnp.float32) + total).astype(jnp.bfloat16)

    @pl.when(moved)
    def _():
        copy = remote(K2 + 6, tsend, acc, (p, f, a))
        copy.start()
        copy.wait()

    @pl.when(jnp.logical_not(moved))
    def _():
        acc[...] = tsend[...]

    out[...] = acc[...]


def fused_body(
    query,
    new_kv,
    kv_pool,
    kv_len,
    mig_dest,
    mig_from,
    mig_to,
    w_out,
    norm_gain,
    w_gate,
    w_up,
    w_down,
    resid,
):
    a = lax.axis_index("attn")
    blocks, bs, kvw = kv_pool.shape
    steps, reqs, qw = query.shape
    rows = steps * reqs
    width = w_out.shape[1]
    units = w_gate.shape[1]
    cu = units // CHUNKS
    qlen = steps * (qw // (kvw // 2))
    entries = mig_dest.shape[0]
    e = jnp.arange(entries, dtype=jnp.int32)
    source = e // (entries // 4)
    key = source * 4 + mig_dest
    earlier = (key[:, None] == key[None, :]) & (e[None, :] < e[:, None])
    rank = jnp.sum(earlier.astype(jnp.int32), axis=1)
    slot = jnp.arange(4 * CAP, dtype=jnp.int32)
    picked = (source == a)[None, :] & ((mig_dest * CAP + rank)[None, :] == slot[:, None])
    sends = jnp.sum(jnp.where(picked, mig_from[None, :], 0), axis=1).astype(jnp.int32)
    block = jnp.arange(blocks, dtype=jnp.int32)
    lands = (mig_dest == a)[None, :] & (mig_to[None, :] == block[:, None])
    table = jnp.maximum(
        block,
        jnp.max(jnp.where(lands, (blocks + source * CAP + rank)[None, :], 0), axis=1),
    ).astype(jnp.int32)

    bf, f32 = jnp.bfloat16, jnp.float32
    smem = pl.BlockSpec(memory_space=pltpu.SMEM)
    vmem = pl.BlockSpec(memory_space=pltpu.VMEM)
    anym = pl.BlockSpec(memory_space=pl.ANY)
    copies = 21 + 5 * CHUNKS + 7
    big = max(w_out.shape[0], w_down.shape[0])
    result = pl.pallas_call(
        layer_kernel,
        out_shape=jax.ShapeDtypeStruct((rows, width), bf),
        in_specs=[smem] * 3 + [vmem] * 4 + [anym] * 5,
        out_specs=vmem,
        scratch_shapes=[
            pltpu.VMEM((blocks + 4 * CAP, bs, kvw), bf),
            pltpu.VMEM((3, CAP, bs, kvw), bf),
            pltpu.VMEM((4 * CAP, bs, kvw), bf),
            pltpu.VMEM((blocks // reqs * bs, kvw), bf),
            pltpu.VMEM((2, reqs * qlen, 128), f32),
            pltpu.VMEM((4, reqs * 16, 128), f32),
            pltpu.VMEM((2, reqs * qlen, 128), f32),
            pltpu.VMEM((4, rows, qw), bf),
            pltpu.VMEM((steps, 4 * reqs, width), f32),
            pltpu.VMEM((4, rows, width), f32),
            pltpu.VMEM((2, 3, rows, width), bf),
            pltpu.VMEM((2, 3, rows, width), bf),
            pltpu.VMEM((4, rows, width), bf),
            pltpu.VMEM((4, rows, width), bf),
            pltpu.VMEM((4, rows, 128), f32),
            pltpu.VMEM((4, rows, 128), f32),
            pltpu.VMEM((big, width), bf),
            pltpu.VMEM((SLOTS, 2, w_gate.shape[0], cu), bf),
            pltpu.VMEM((2, 4, rows, 2 * cu), f32),
            pltpu.VMEM((CHUNKS, 2, rows, 2 * cu), bf),
            pltpu.VMEM((CHUNKS, 2, rows, 2 * cu), bf),
            pltpu.VMEM((CHUNKS, rows, 2 * cu), bf),
            pltpu.VMEM((CHUNKS, rows, 2 * cu), bf),
            pltpu.VMEM((CHUNKS, 4, rows, cu), bf),
            pltpu.VMEM((rows, width), bf),
            pltpu.VMEM((rows, width), bf),
            pltpu.SemaphoreType.DMA((2 + 2 * SLOTS,)),
            pltpu.SemaphoreType.DMA((copies,)),
            pltpu.SemaphoreType.DMA((copies,)),
        ],
        compiler_params=pltpu.CompilerParams(
            collective_id=0, has_side_effects=True, vmem_limit_bytes=60 * 1024 * 1024
        ),
    )(
        table,
        sends,
        kv_len,
        query,
        new_kv,
        resid,
        norm_gain.reshape(1, -1),
        kv_pool,
        w_out,
        w_gate,
        w_up,
        w_down,
    )
    return result.reshape(steps, reqs, width)


def solution(mesh):
    placed = (
        P(None, ("parts", "attn"), "ffn"),
        P(None, ("parts", "attn"), None),
        P(("parts", "attn"), None, None),
        P(("parts", "attn")),
        P("parts"),
        P("parts"),
        P("parts"),
        P("ffn", "attn"),
        P("attn"),
        P("attn", "ffn"),
        P("attn", "ffn"),
        P("ffn", "attn"),
        P(None, "parts", "attn"),
    )
    use_kernel = mesh.shape["attn"] == 4 and mesh.shape["ffn"] == 4
    return jax.shard_map(
        fused_body if use_kernel else body,
        mesh=mesh,
        in_specs=placed,
        out_specs=P(None, ("parts", "attn"), "ffn"),
        check_vma=False,
    )
```

```python
import jax
import jax.numpy as jnp
from jax import lax
from jax.experimental import pallas as pl
from jax.experimental.pallas import tpu as pltpu
from jax.sharding import PartitionSpec as P

D = 7168
CAP = 2
STEPS = 4


def stored(value):
    return lax.optimization_barrier(value.astype(jnp.bfloat16)).astype(jnp.float32)


def attend_local(queries, cache_kv, lengths, fresh_kv, head_dim):
    row_count = queries.shape[0]
    per_head = queries.reshape(row_count, -1, head_dim)
    key_part = cache_kv[:, :, :head_dim]
    value_part = cache_kv[:, :, head_dim:]
    score_scale = head_dim ** (-0.5)
    cache_scores = (
        jnp.einsum("rhd,rcd->rhc", per_head, key_part, preferred_element_type=jnp.float32)
        * score_scale
    )
    position = jnp.arange(cache_kv.shape[1], dtype=jnp.int32)
    live_mask = position[None, None, :] < lengths[:, None, None]
    cache_scores = jnp.where(live_mask, cache_scores, -jnp.inf)
    fresh_keys = fresh_kv[:, :, :head_dim]
    fresh_values = fresh_kv[:, :, head_dim:]
    recent_scores = (
        jnp.einsum("rhd,srd->rhs", per_head, fresh_keys, preferred_element_type=jnp.float32)
        * score_scale
    )
    row_max = jnp.maximum(jnp.max(cache_scores, axis=2), jnp.max(recent_scores, axis=2))
    cache_probs = jnp.exp(cache_scores - row_max[:, :, None])
    recent_probs = jnp.exp(recent_scores - row_max[:, :, None])
    weight_sum = jnp.sum(cache_probs, axis=2) + jnp.sum(recent_probs, axis=2)
    weighted = jnp.einsum(
        "rhc,rcd->rhd",
        cache_probs.astype(jnp.bfloat16),
        value_part,
        preferred_element_type=jnp.float32,
    )
    weighted = weighted + jnp.einsum(
        "rhs,srd->rhd",
        recent_probs.astype(jnp.bfloat16),
        fresh_values,
        preferred_element_type=jnp.float32,
    )
    return (weighted / weight_sum[:, :, None]).astype(jnp.bfloat16).reshape(row_count, -1)


def body(
    query,
    new_kv,
    kv_pool,
    kv_len,
    mig_dest,
    mig_from,
    mig_to,
    w_out,
    norm_gain,
    w_gate,
    w_up,
    w_down,
    resid,
):
    peer_count = lax.axis_size("attn")
    my_index = lax.axis_index("attn")
    blocks = kv_pool.shape[0]
    feature_width = kv_pool.shape[2]
    entries = mig_dest.shape[0]
    per_source = entries // peer_count
    entry_index = jnp.arange(entries, dtype=jnp.int32)
    source = entry_index // per_source
    pair_key = source * peer_count + mig_dest
    earlier = (pair_key[:, None] == pair_key[None, :]) & (
        entry_index[None, :] < entry_index[:, None]
    )
    pair_rank = jnp.sum(earlier.astype(jnp.int32), axis=1)
    my_dest = lax.dynamic_slice_in_dim(mig_dest, my_index * per_source, per_source)
    my_from = lax.dynamic_slice_in_dim(mig_from, my_index * per_source, per_source)
    my_rank = lax.dynamic_slice_in_dim(pair_rank, my_index * per_source, per_source)
    send_slot = my_dest * CAP + my_rank
    outgoing = jnp.zeros((peer_count * CAP, kv_pool.shape[1], feature_width), jnp.bfloat16)
    outgoing = (
        outgoing.at[send_slot]
        .set(kv_pool[my_from])
        .reshape(peer_count, CAP, kv_pool.shape[1], feature_width)
    )
    land_slot = jnp.where(mig_dest == my_index, source * CAP + pair_rank, peer_count * CAP)
    landing = (
        jnp.full((peer_count * CAP,), blocks, jnp.int32).at[land_slot].set(mig_to, mode="drop")
    )
    arrived = lax.all_to_all(outgoing, "attn", split_axis=0, concat_axis=0, tiled=True)
    received = arrived.reshape(peer_count * CAP, kv_pool.shape[1], feature_width)
    new_pool = kv_pool.at[landing].set(received, mode="drop")
    cache_kv = new_pool.reshape(kv_len.shape[0], -1, feature_width)
    head_dim = feature_width // 2
    paired = jnp.concatenate([w_gate, w_up], axis=1)
    unit_count = w_gate.shape[1]
    lane_count = lax.axis_size("ffn")
    lane_index = lax.axis_index("ffn")
    outputs = []
    for decode_step in range(STEPS):
        attended = attend_local(
            query[decode_step], cache_kv, kv_len, new_kv[: decode_step + 1], head_dim
        )
        head_part = jnp.dot(
            lax.all_gather(attended, "attn", axis=0, tiled=True),
            w_out,
            preferred_element_type=jnp.float32,
        ).astype(jnp.bfloat16)
        head_sum = lax.psum(head_part.astype(jnp.float32).astype(jnp.bfloat16), "ffn").astype(
            jnp.float32
        )
        state_bf = (resid[decode_step].astype(jnp.float32) + head_sum).astype(jnp.bfloat16)
        widened = state_bf.astype(jnp.float32)
        squares = lax.psum(jnp.sum(widened * widened, axis=1), "attn")
        normed = (
            widened * lax.rsqrt(squares[:, None] / D + 1e-06) * norm_gain.astype(jnp.float32)
        ).astype(jnp.bfloat16)
        gate_up = lax.psum_scatter(
            stored(jnp.dot(normed, paired, preferred_element_type=jnp.float32)).astype(
                jnp.bfloat16
            ),
            "attn",
            scatter_dimension=0,
            tiled=True,
        ).astype(jnp.float32)
        hidden = (jax.nn.silu(gate_up[:, :unit_count]) * gate_up[:, unit_count:]).astype(
            jnp.bfloat16
        )
        unit_part = jnp.dot(
            lax.all_gather(hidden, "attn", axis=0, tiled=True),
            w_down,
            preferred_element_type=jnp.float32,
        ).astype(jnp.bfloat16)
        unit_sum = lax.psum(unit_part.astype(jnp.float32).astype(jnp.bfloat16), "ffn").astype(
            jnp.float32
        )
        layer_out = (widened + unit_sum).astype(jnp.bfloat16)
        by_row = lax.all_to_all(layer_out, "attn", split_axis=0, concat_axis=1, tiled=True)
        share_width = by_row.shape[1] // lane_count
        outputs.append(lax.dynamic_slice_in_dim(by_row, lane_index * share_width, share_width, 1))
    return jnp.stack(outputs)


MESH = pl.DeviceIdType.MESH
CHUNKS = 6
SLOTS = 4
PAIR = 2
KEEP = 3
COLS = 256


def near_of(i):
    return i + 1 - 2 * lax.rem(i, 2)


def far_of(i):
    return lax.rem(i + 2, 4)


def layer_kernel(
    mig_dest,
    mig_from,
    mig_to,
    lengths,
    query,
    new_kv,
    resid,
    gain,
    pool_hbm,
    w_out,
    w_gate,
    w_up,
    w_down,
    out,
    pool,
    stage,
    land,
    cache,
    q_rows,
    fresh,
    att_rows,
    att,
    wide,
    part,
    zsend,
    zrecv,
    state,
    lhs,
    sq_send,
    sq_recv,
    wbig,
    wgu,
    gu_keep,
    gu_send,
    gu_recv,
    gx_send,
    gx_recv,
    hid,
    acc,
    tsend,
    lsem,
    ssem,
    rsem,
):
    a = lax.axis_index("attn")
    f = lax.axis_index("ffn")
    p = lax.axis_index("parts")
    an, af = near_of(a), far_of(a)
    fn, ff = near_of(f), far_of(f)
    aff, fff = far_of(an), far_of(fn)
    blocks = pool_hbm.shape[0]
    reqs = lengths.shape[0]
    steps = query.shape[0]
    rows = steps * reqs
    hd = pool_hbm.shape[2] // 2
    heads = query.shape[2] // hd
    qlen = steps * heads
    width = w_out.shape[1]
    units = w_gate.shape[1]
    cu = units // CHUNKS
    per_req = blocks // reqs
    bs = pool_hbm.shape[1]

    def at_attn(i):
        return (p, i, f)

    def at_ffn(i):
        return (p, a, i)

    def remote(k, src, dst, dev):
        return pltpu.make_async_remote_copy(
            src_ref=src,
            dst_ref=dst,
            send_sem=ssem.at[k],
            recv_sem=rsem.at[k],
            device_id=dev,
            device_id_type=MESH,
        )

    def gu_load(c):
        s = c % SLOTS
        return [
            pltpu.make_async_copy(
                w.at[:, pl.ds(c * cu, cu)], wgu.at[s, j], lsem.at[2 + s * 2 + j]
            )
            for j, w in enumerate((w_gate, w_up))
        ]

    pool_load = pltpu.make_async_copy(pool_hbm, pool.at[pl.ds(0, blocks)], lsem.at[0])
    pool_load.start()
    out_load = pltpu.make_async_copy(w_out, wbig.at[pl.ds(0, w_out.shape[0])], lsem.at[1])

    barrier = pltpu.get_barrier_semaphore()
    moved = a != f
    for o in range(1, 4):
        pl.semaphore_signal(
            barrier, inc=1, device_id=at_attn(lax.rem(a + o, 4)), device_id_type=MESH
        )
    for peer in (fn, ff):
        pl.semaphore_signal(barrier, inc=1, device_id=at_ffn(peer), device_id_type=MESH)

    @pl.when(moved)
    def _():
        pl.semaphore_signal(barrier, inc=1, device_id=(p, f, a), device_id_type=MESH)
        pl.semaphore_wait(barrier, 6)

    @pl.when(jnp.logical_not(moved))
    def _():
        pl.semaphore_wait(barrier, 5)

    per_source = mig_dest.shape[0] // 4

    def entry_of(source, dest, rank, values, none):
        seen = jnp.int32(0)
        found = jnp.int32(none)
        for e in range(per_source):
            here = mig_dest[source * per_source + e] == dest
            hit = jnp.logical_and(here, seen == rank)
            found = jnp.where(hit, values[source * per_source + e], found)
            seen = seen + jnp.where(here, 1, 0)
        return found

    pool_load.wait()
    mig = []
    for o in range(1, 4):
        d = lax.rem(a + o, 4)
        for s in range(CAP):
            stage[o - 1, s] = pool[entry_of(a, d, s, mig_from, 0)]
        mig.append(
            remote(o - 1, stage.at[o - 1], land.at[pl.ds(CAP * a, CAP)], at_attn(d))
        )
        mig[-1].start()
    out_load.start()
    for c in range(SLOTS):
        for d in gu_load(c):
            d.start()

    for t in range(steps):
        q_t = query[t].astype(jnp.float32)
        for h in range(heads):
            for half in range(2):
                lo = h * hd + half * 128
                q_rows[half, pl.ds(t * heads + h, reqs, stride=qlen), :] = q_t[:, lo : lo + 128]
    fresh[...] = jnp.zeros_like(fresh)
    for t in range(steps):
        fresh_t = new_kv[t].astype(jnp.float32)
        for half in range(4):
            fresh[half, pl.ds(t, reqs, stride=16), :] = fresh_t[:, half * 128 : (half + 1) * 128]
    for t in range(steps):
        wide[t] = resid[t].astype(jnp.float32)

    land[pl.ds(CAP * a, CAP)] = jnp.zeros((CAP, bs, 2 * hd), jnp.bfloat16)
    for copy in mig:
        copy.wait()
    pool[pl.ds(blocks, 4 * CAP)] = land[...]

    landed = []
    for o in range(1, 4):
        source = lax.rem(a + o, 4)
        for s in range(CAP):
            landed.append((entry_of(source, a, s, mig_to, -1), blocks + CAP * source + s))

    scale = hd ** (-0.5)

    contract = (((1,), (1,)), ((), ()))

    def score(i, u):
        for b in range(per_req):
            block = i * per_req + b
            index = block
            for to, slot in landed:
                index = jnp.where(to == block, slot, index)
            cache[u, b * bs : (b + 1) * bs, :] = pool[index]
        mine = pl.ds(i * qlen, qlen)
        q = jnp.concatenate([q_rows[0, mine, :], q_rows[1, mine, :]], axis=1).astype(jnp.bfloat16)
        s1 = lax.dot_general(q, cache[u, :, :hd], contract, preferred_element_type=jnp.float32)
        at = pl.ds(i * 16, 16)
        fk = jnp.concatenate([fresh[0, at, :], fresh[1, at, :]], axis=1).astype(jnp.bfloat16)
        s2 = lax.dot_general(q, fk, contract, preferred_element_type=jnp.float32)
        return s1 * scale, s2 * scale

    def softmax(i, s1, s2):
        pos = lax.broadcasted_iota(jnp.int32, s1.shape, 1)
        s1 = jnp.where(pos < lengths[i], s1, -jnp.inf)
        step_of = lax.broadcasted_iota(jnp.int32, s2.shape, 0) // heads
        s2 = jnp.where(lax.broadcasted_iota(jnp.int32, s2.shape, 1) <= step_of, s2, -jnp.inf)
        top = jnp.maximum(
            jnp.max(s1, axis=1, keepdims=True), jnp.max(s2, axis=1, keepdims=True)
        )
        p1 = jnp.exp(s1 - top)
        p2 = jnp.exp(s2 - top)
        total = jnp.sum(p1, axis=1, keepdims=True) + jnp.sum(p2, axis=1, keepdims=True)
        return p1.astype(jnp.bfloat16), p2.astype(jnp.bfloat16), total

    def attend(i, u, p1, p2, total):
        at = pl.ds(i * 16, 16)
        fv = jnp.concatenate([fresh[2, at, :], fresh[3, at, :]], axis=1).astype(jnp.bfloat16)
        o = jnp.dot(p1, cache[u, :, hd:], preferred_element_type=jnp.float32) + jnp.dot(
            p2, fv, preferred_element_type=jnp.float32
        )
        return o / total

    def request_pair(k, carry):
        first = k * PAIR
        scored = [score(first + u, u) for u in range(PAIR)]
        probs = [softmax(first + u, *scored[u]) for u in range(PAIR)]
        outs = [attend(first + u, u, *probs[u]) for u in range(PAIR)]
        for u in range(PAIR):
            for half in range(2):
                att_rows[half, pl.ds((first + u) * qlen, qlen), :] = outs[u][
                    :, half * 128 : (half + 1) * 128
                ]
        return carry

    lax.fori_loop(0, reqs // PAIR, request_pair, 0)

    def lay_out(first, last):
        for h in range(first, last):
            for half in range(2):
                lo = h * hd + half * 128
                att[a, :, lo : lo + 128] = jnp.concatenate(
                    [
                        att_rows[half, pl.ds(t * heads + h, reqs, stride=qlen), :]
                        for t in range(steps)
                    ],
                    axis=0,
                ).astype(jnp.bfloat16)

    def gather_begin(k, at, me, near, far, dev):
        own = [remote(k + 1, at(me), at(me), dev(far)), remote(k, at(me), at(me), dev(near))]
        for copy in own:
            copy.start()
        return own

    def gather_relay(k, own, at, near, far, dev):
        own[0].wait_recv()
        relay = remote(k + 2, at(far), at(far), dev(near))
        relay.start()
        return own + [relay]

    def gather_end(copies):
        copies[1].wait_recv()
        copies[2].wait_recv()
        for copy in copies:
            copy.wait_send()

    kh = heads // 2 * hd

    def att_at(part_index):
        return lambda i: att.at[i, :, pl.ds(part_index * kh, kh)]

    lay_out(0, heads // 2)
    a0 = gather_begin(3, att_at(0), a, an, af, at_attn)
    lay_out(heads // 2, heads)
    a1 = gather_begin(18 + 3, att_at(1), a, an, af, at_attn)
    a0 = gather_relay(3, a0, att_at(0), an, af, at_attn)
    out_load.wait()
    gather_end(a0)

    tiles = width // COLS
    half_tiles = ((tiles + 1) // 2, tiles // 2)
    col_cuts = ((0, half_tiles[0] * COLS), (half_tiles[0] * COLS, width))

    def out_tile(j, carry):
        at = pl.ds(pl.multiple_of(j * COLS, COLS), COLS)
        r = jnp.dot(
            att[:, :, :kh].reshape(4 * rows, kh),
            wbig[:kh, at],
            preferred_element_type=jnp.float32,
        )
        part[:, :, at] = r.reshape(4, rows, COLS)
        return carry

    def out_tile_rest(j, carry):
        at = pl.ds(pl.multiple_of(j * COLS, COLS), COLS)
        r = jnp.dot(
            att[:, :, kh:].reshape(4 * rows, kh),
            wbig[kh : 2 * kh, at],
            preferred_element_type=jnp.float32,
        )
        part[:, :, at] = part[:, :, at] + r.reshape(4, rows, COLS)
        return carry

    def reduce_near(k, z, lo, hi):
        zsend[z, 0, :, lo:hi] = part[fff, :, lo:hi].astype(jnp.bfloat16)
        zsend[z, 1, :, lo:hi] = part[fn, :, lo:hi].astype(jnp.bfloat16)
        copies = []
        for j in range(2):
            piece = (z, j, slice(None), pl.ds(lo, hi - lo))
            copies.append(remote(k + j, zsend.at[piece], zrecv.at[piece], at_ffn(fn)))
            copies[-1].start()
        return copies

    def reduce_far(k, z, lo, hi, copies):
        copies[0].wait_recv()
        zsend[z, 2, :, lo:hi] = (
            part[ff, :, lo:hi] + zrecv[z, 0, :, lo:hi].astype(jnp.float32)
        ).astype(jnp.bfloat16)
        piece = (z, 2, slice(None), pl.ds(lo, hi - lo))
        copy = remote(k + 2, zsend.at[piece], zrecv.at[piece], at_ffn(ff))
        copy.start()
        return copies + [copy]

    def reduce_end(z, lo, hi, copies):
        copies[1].wait_recv()
        copies[2].wait_recv()
        total = (
            part[f, :, lo:hi]
            + zrecv[z, 1, :, lo:hi].astype(jnp.float32)
            + zrecv[z, 2, :, lo:hi].astype(jnp.float32)
        )
        for copy in copies:
            copy.wait_send()
        return total

    def state_at(lo, hi):
        return lambda i: state.at[i, :, pl.ds(lo, hi - lo)]

    def make_state(lo, hi, total):
        base = jnp.concatenate(
            [wide[t, pl.ds(pl.multiple_of(f * reqs, reqs), reqs), lo:hi] for t in range(steps)],
            axis=0,
        )
        state[f, :, lo:hi] = (base + total).astype(jnp.bfloat16)

    (l0, h0), (l1, h1) = col_cuts
    lax.fori_loop(0, half_tiles[0], out_tile, 0)
    a1 = gather_relay(18 + 3, a1, att_at(1), an, af, at_attn)
    lax.fori_loop(half_tiles[0], tiles, out_tile, 0)
    gather_end(a1)
    lax.fori_loop(0, half_tiles[0], out_tile_rest, 0)
    r0 = reduce_near(6, 0, l0, h0)
    lax.fori_loop(half_tiles[0], tiles, out_tile_rest, 0)
    down_load = pltpu.make_async_copy(w_down, wbig, lsem.at[1])
    down_load.start()
    r1 = reduce_near(9, 0, l1, h1)
    r0 = reduce_far(6, 0, l0, h0, r0)
    r1 = reduce_far(9, 0, l1, h1, r1)
    make_state(l0, h0, reduce_end(0, l0, h0, r0))
    g0 = gather_begin(12, state_at(l0, h0), f, fn, ff, at_ffn)
    make_state(l1, h1, reduce_end(0, l1, h1, r1))
    g1 = gather_begin(15, state_at(l1, h1), f, fn, ff, at_ffn)
    g0 = gather_relay(12, g0, state_at(l0, h0), fn, ff, at_ffn)
    g1 = gather_relay(15, g1, state_at(l1, h1), fn, ff, at_ffn)
    gather_end(g0)
    gather_end(g1)

    gain_f = gain[...].astype(jnp.float32).reshape(1, width)

    def scale_rows(i, carry):
        w = state[i].astype(jnp.float32)
        lhs[i] = (w * gain_f).astype(jnp.bfloat16)
        sq_send[i] = jnp.broadcast_to(jnp.sum(w * w, axis=1, keepdims=True), (rows, 128))
        return carry

    lax.fori_loop(0, 4, scale_rows, 0)
    sq = []
    for o in range(1, 4):
        d = lax.rem(a + o, 4)
        sq.append(remote(17 + o, sq_send.at[d], sq_recv.at[a], at_attn(d)))
        sq[-1].start()
    sq_recv[a] = sq_send[a]

    K = 24
    near_copy, far_copy, hid_copy = {}, {}, {}

    def hid_at(c):
        return lambda i: hid.at[c, i]

    def stage_matmul(c):
        s = c % SLOTS
        for d in gu_load(c):
            d.wait()

        for j in range(2):

            def tile(n, carry):
                at = pl.ds(pl.multiple_of(n * COLS, COLS), COLS)
                to = pl.ds(pl.multiple_of(j * cu + n * COLS, COLS), COLS)
                gu_keep[c % KEEP, :, :, to] = jnp.dot(
                    lhs[...].reshape(4 * rows, width),
                    wgu[s, j, :, at],
                    preferred_element_type=jnp.float32,
                ).reshape(4, rows, COLS)
                return carry

            lax.fori_loop(0, cu // COLS, tile, 0)
        if c + SLOTS < CHUNKS:
            for d in gu_load(c + SLOTS):
                d.start()
        gu_send[c, 0] = gu_keep[c % KEEP, aff].astype(jnp.bfloat16)
        gu_send[c, 1] = gu_keep[c % KEEP, an].astype(jnp.bfloat16)
        near_copy[c] = remote(K + c, gu_send.at[c], gu_recv.at[c], at_attn(an))
        near_copy[c].start()

    def stage_far(c):
        near_copy[c].wait()
        gx_send[c] = (gu_keep[c % KEEP, af] + gu_recv[c, 0].astype(jnp.float32)).astype(
            jnp.bfloat16
        )
        far_copy[c] = remote(K + CHUNKS + c, gx_send.at[c], gx_recv.at[c], at_attn(af))
        far_copy[c].start()
        gu_keep[c % KEEP, a] = gu_keep[c % KEEP, a] + gu_recv[c, 1].astype(jnp.float32)

    def stage_hidden(c, rs):
        far_copy[c].wait()
        gu = gu_keep[c % KEEP, a] + gx_recv[c].astype(jnp.float32)
        g = gu[:, :cu] * rs
        u = gu[:, cu:] * rs
        hid[c, a] = (g / (1.0 + jnp.exp(-g)) * u).astype(jnp.bfloat16)
        hid_copy[c] = gather_begin(K + 2 * CHUNKS + 3 * c, hid_at(c), a, an, af, at_attn)

    def stage_relay(c):
        hid_copy[c] = gather_relay(
            K + 2 * CHUNKS + 3 * c, hid_copy[c], hid_at(c), an, af, at_attn
        )

    def stage_down(c, first, last):
        if first == 0:
            gather_end(hid_copy[c])

        def tile(n, carry):
            at = pl.ds(pl.multiple_of(n * COLS, COLS), COLS)
            r = jnp.dot(
                hid[c].reshape(4 * rows, cu),
                wbig[c * cu : (c + 1) * cu, at],
                preferred_element_type=jnp.float32,
            ).reshape(4, rows, COLS)
            if c == 0:
                part[:, :, at] = r
            else:
                part[:, :, at] = part[:, :, at] + r
            return carry

        lax.fori_loop(first, last, tile, 0)

    stage_matmul(0)
    for copy in sq:
        copy.wait()
    squares = sq_recv[0] + sq_recv[1] + sq_recv[2] + sq_recv[3]
    rs = lax.rsqrt(squares[:, :1] / D + 1e-06)
    for c in range(1, CHUNKS + 4):
        if c < CHUNKS:
            stage_matmul(c)
        if c - 1 < CHUNKS:
            stage_far(c - 1)
        if 0 <= c - 2 < CHUNKS:
            stage_hidden(c - 2, rs)
        if 0 <= c - 3 < CHUNKS:
            stage_relay(c - 3)
        if c == 4:
            down_load.wait()
        if 0 <= c - 4 < CHUNKS - 1:
            stage_down(c - 4, 0, tiles)

    K2 = K + 5 * CHUNKS
    stage_down(CHUNKS - 1, 0, half_tiles[0])
    d0 = reduce_near(K2, 1, l0, h0)
    stage_down(CHUNKS - 1, half_tiles[0], tiles)
    d1 = reduce_near(K2 + 3, 1, l1, h1)
    d0 = reduce_far(K2, 1, l0, h0, d0)
    d1 = reduce_far(K2 + 3, 1, l1, h1, d1)
    def turn(k, lo, hi):
        at = (slice(None), pl.ds(lo, hi - lo))
        return remote(k, tsend.at[at], acc.at[at], (p, f, a))

    for k, lo, hi, d in ((K2 + 6, l0, h0, d0), (K2 + 7, l1, h1, d1)):
        total = reduce_end(1, lo, hi, d)
        tsend[:, lo:hi] = (state[f, :, lo:hi].astype(jnp.float32) + total).astype(jnp.bfloat16)

        @pl.when(moved)
        def _():
            turn(k, lo, hi).start()

    @pl.when(moved)
    def _():
        turn(K2 + 6, l0, h0).wait()
        turn(K2 + 7, l1, h1).wait()

    @pl.when(jnp.logical_not(moved))
    def _():
        acc[...] = tsend[...]

    out[...] = acc[...].astype(jnp.float32).reshape(steps, reqs, width).astype(jnp.bfloat16)


def fused_body(
    query,
    new_kv,
    kv_pool,
    kv_len,
    mig_dest,
    mig_from,
    mig_to,
    w_out,
    norm_gain,
    w_gate,
    w_up,
    w_down,
    resid,
):
    blocks, bs, kvw = kv_pool.shape
    steps, reqs, qw = query.shape
    rows = steps * reqs
    width = w_out.shape[1]
    units = w_gate.shape[1]
    cu = units // CHUNKS
    qlen = steps * (qw // (kvw // 2))
    bf, f32 = jnp.bfloat16, jnp.float32
    smem = pl.BlockSpec(memory_space=pltpu.SMEM)
    vmem = pl.BlockSpec(memory_space=pltpu.VMEM)
    anym = pl.BlockSpec(memory_space=pl.ANY)
    copies = 24 + 5 * CHUNKS + 8
    big = max(w_out.shape[0], w_down.shape[0])
    result = pl.pallas_call(
        layer_kernel,
        out_shape=jax.ShapeDtypeStruct((steps, reqs, width), bf),
        in_specs=[smem] * 4 + [vmem] * 4 + [anym] * 5,
        out_specs=vmem,
        scratch_shapes=[
            pltpu.VMEM((blocks + 4 * CAP, bs, kvw), bf),
            pltpu.VMEM((3, CAP, bs, kvw), bf),
            pltpu.VMEM((4 * CAP, bs, kvw), bf),
            pltpu.VMEM((PAIR, blocks // reqs * bs, kvw), bf),
            pltpu.VMEM((2, reqs * qlen, 128), f32),
            pltpu.VMEM((4, reqs * 16, 128), f32),
            pltpu.VMEM((2, reqs * qlen, 128), f32),
            pltpu.VMEM((4, rows, qw), bf),
            pltpu.VMEM((steps, 4 * reqs, width), f32),
            pltpu.VMEM((4, rows, width), f32),
            pltpu.VMEM((2, 3, rows, width), bf),
            pltpu.VMEM((2, 3, rows, width), bf),
            pltpu.VMEM((4, rows, width), bf),
            pltpu.VMEM((4, rows, width), bf),
            pltpu.VMEM((4, rows, 128), f32),
            pltpu.VMEM((4, rows, 128), f32),
            pltpu.VMEM((big, width), bf),
            pltpu.VMEM((SLOTS, 2, w_gate.shape[0], cu), bf),
            pltpu.VMEM((KEEP, 4, rows, 2 * cu), f32),
            pltpu.VMEM((CHUNKS, 2, rows, 2 * cu), bf),
            pltpu.VMEM((CHUNKS, 2, rows, 2 * cu), bf),
            pltpu.VMEM((CHUNKS, rows, 2 * cu), bf),
            pltpu.VMEM((CHUNKS, rows, 2 * cu), bf),
            pltpu.VMEM((CHUNKS, 4, rows, cu), bf),
            pltpu.VMEM((rows, width), bf),
            pltpu.VMEM((rows, width), bf),
            pltpu.SemaphoreType.DMA((2 + 2 * SLOTS,)),
            pltpu.SemaphoreType.DMA((copies,)),
            pltpu.SemaphoreType.DMA((copies,)),
        ],
        compiler_params=pltpu.CompilerParams(
            collective_id=0, has_side_effects=True, vmem_limit_bytes=60 * 1024 * 1024
        ),
    )(
        mig_dest,
        mig_from,
        mig_to,
        kv_len,
        query,
        new_kv,
        resid,
        norm_gain,
        kv_pool,
        w_out,
        w_gate,
        w_up,
        w_down,
    )
    return result


def solution(mesh):
    placed = (
        P(None, ("parts", "attn"), "ffn"),
        P(None, ("parts", "attn"), None),
        P(("parts", "attn"), None, None),
        P(("parts", "attn")),
        P("parts"),
        P("parts"),
        P("parts"),
        P("ffn", "attn"),
        P("attn"),
        P("attn", "ffn"),
        P("attn", "ffn"),
        P("ffn", "attn"),
        P(None, "parts", "attn"),
    )
    use_kernel = mesh.shape["attn"] == 4 and mesh.shape["ffn"] == 4
    return jax.shard_map(
        fused_body if use_kernel else body,
        mesh=mesh,
        in_specs=placed,
        out_specs=P(None, ("parts", "attn"), "ffn"),
        check_vma=False,
    )
```
